32 devices in a mesh: gx: 8 (over y, x, core), gy: 4 (over z).
Axes of the slice: x: 2, y: 2, z: 4, core: 2. Of those that a mesh axis runs over, the one named last changes fastest.
Arguments:
- water_state: float32 [3, 512, 2048], P(None, 'gy', 'gx'), may hold values from -0.5 to 1.5, as said below
- bed_level: float32 [512, 2048], P('gy', 'gx'), may hold values from -0.1 to 0.1
- active_tiles: int32 [1, 4, 16], replicated, may hold values from 0 to 1, as said below
- roughness: int32 [4, 16], replicated, may hold values from 0 to 3
Outputs:
- water_out: float32 [3, 512, 2048], P(None, 'gy', 'gx')
The draws below stay inside these ranges and needn't reach their ends.
Inputs may be any that keep to these rules, and one draw needn't show every extreme that they name: `water_state`: entry 0 along the first dimension is the water depth, at least 0.5 everywhere; entries 1 and 2 are the discharges along the columns and along the rows, of magnitude at most 0.5. `active_tiles`: whole blocks of 2 tiles side by side along the columns, starting at multiples of 2, may be off the list together.
All inputs are finite; a program needn't handle non-finite values.
Results may differ from the reference program's by a relative error of at most 0.0003.
Values sent between devices are 32-bit elements; how exact they have to be, the bound alone decides.
A program may use at most 64 MiB of HBM per device.

```python
import jax
import jax.numpy as jnp
from jax import lax

TILE = 128
TX_DEV = 2
SUBSTEPS = 1
NY = 512
NX = 2048
NTY = 4
NTX = 16


def draw_water_state(key, part):
    depth_key, flow_key = jax.random.split(key, 2)
    water_depth = jax.random.uniform(depth_key, (NY, NX), jnp.float32, 0.5, 1.5)
    discharge = jax.random.uniform(flow_key, (2, NY, NX), jnp.float32, -0.5, 0.5)
    return jnp.concatenate([water_depth[None], discharge], axis=0)


def draw_active_tiles(key, part):
    block_key, tile_key = jax.random.split(jax.random.fold_in(key, 7))
    block_wet = jax.random.randint(block_key, (SUBSTEPS, NTY, NTX // TX_DEV, 1), 0, 5) < 3
    tile_wet = jax.random.randint(tile_key, (SUBSTEPS, NTY, NTX // TX_DEV, TX_DEV), 0, 4) > 0
    return (block_wet & tile_wet).reshape(SUBSTEPS, NTY, NTX).astype(jnp.int32)


def place_ends(values, own_key, low, top_value):
    longest = values.shape.index(max(values.shape))
    spots = []
    for shift in (0, 1):
        where = [jax.random.randint(jax.random.fold_in(own_key, axis), (), 0, length) for axis, length in enumerate(values.shape)]
        where[longest] = (where[longest] + shift) % values.shape[longest]
        spots.append(tuple(where))
    return values.at[spots[0]].set(low).at[spots[1]].set(top_value)


def levels(stream_key, extent, shards, least, high):
    factor_of, own = 1.0, jax.random.fold_in(stream_key, 6)
    for dim, parts in shards:
        heights = jnp.exp(jax.random.uniform(jax.random.fold_in(own, dim), (parts,), jnp.float32, least / len(shards), high / len(shards)))
        factor_of = factor_of * jnp.repeat(heights, extent[dim] // parts).reshape([-1 if axis == dim else 1 for axis in range(len(extent))])
    return factor_of


def setup_inputs(seed: int = 0) -> dict:
    splits = jax.random.split(jax.random.key(seed), 5)
    water_state = draw_water_state(jax.random.fold_in(splits[4], 71), 0)
    bed_level = jnp.clip(jax.random.uniform(splits[1], (NY, NX), jnp.float32, -0.1, 0.1) * levels(splits[1], (NY, NX), ((0, 4), (1, 8)), -0.4, 0.0), -0.1, 0.1)
    active_tiles = draw_active_tiles(jax.random.fold_in(splits[4], 71), 0)
    roughness = place_ends(jax.random.randint(splits[3], (NTY, NTX), 0, 4), jax.random.fold_in(splits[3], 1), 0, 3).astype(jnp.int32)
    return dict(water_state=water_state, bed_level=bed_level, active_tiles=active_tiles, roughness=roughness)


GRAVITY = 9.81
SPACING = 2.0
TIME_STEP = 0.1
MANNING = (0.03, 0.06, 0.1, 0.15)
ROW_SIGNS = (1.0, 1.0, -1.0)
COL_SIGNS = (1.0, -1.0, 1.0)

def minmod_limit(lower, upper):
    return jnp.where(lower * upper > 0.0, jnp.sign(lower) * jnp.minimum(jnp.abs(lower), jnp.abs(upper)), 0.0)

def cut_along(array, begin, finish, axis):
    return lax.slice_in_dim(array, begin, finish, axis=axis)

def face_states(field, axis, interior):
    between = cut_along(field, 1, interior + 4, axis) - cut_along(field, 0, interior + 3, axis)
    slopes = minmod_limit(cut_along(between, 0, interior + 2, axis), cut_along(between, 1, interior + 3, axis))
    left_side = cut_along(field, 1, interior + 2, axis) + 0.5 * cut_along(slopes, 0, interior + 1, axis)
    right_side = cut_along(field, 2, interior + 3, axis) - 0.5 * cut_along(slopes, 1, interior + 2, axis)
    return (left_side, right_side)

def physical_flux(water_depth, normal_flow, tangent_flow):
    velocity = normal_flow / water_depth
    fluxes = (normal_flow, normal_flow * velocity + 0.5 * GRAVITY * water_depth * water_depth, tangent_flow * velocity)
    return (fluxes, jnp.abs(velocity) + jnp.sqrt(GRAVITY * water_depth))

def rusanov_flux(left_side, right_side):
    left_flux, left_speed = physical_flux(*left_side)
    right_flux, right_speed = physical_flux(*right_side)
    fastest = jnp.maximum(left_speed, right_speed)
    return tuple((0.5 * (a + b) - 0.5 * fastest * (r - l) for a, b, l, r in zip(left_flux, right_flux, left_side, right_side)))

def tendency(extended, bed_part, friction, active, row_count, col_count):
    water_depth, flow_x, flow_y = (extended[0], extended[1], extended[2])
    across = [face_states(f[2:row_count + 2, :], 1, col_count) for f in (water_depth, flow_x, flow_y)]
    flux_x = rusanov_flux(tuple((p[0] for p in across)), tuple((p[1] for p in across)))
    downward = [face_states(f[:, 2:col_count + 2], 0, row_count) for f in (water_depth, flow_y, flow_x)]
    flux_y = rusanov_flux(tuple((p[0] for p in downward)), tuple((p[1] for p in downward)))
    centre_depth = water_depth[2:row_count + 2, 2:col_count + 2]
    centre_x = flow_x[2:row_count + 2, 2:col_count + 2]
    centre_y = flow_y[2:row_count + 2, 2:col_count + 2]
    slope_x = (bed_part[2:row_count + 2, 3:col_count + 3] - bed_part[2:row_count + 2, 1:col_count + 1]) / (2.0 * SPACING)
    slope_y = (bed_part[3:row_count + 3, 2:col_count + 2] - bed_part[1:row_count + 1, 2:col_count + 2]) / (2.0 * SPACING)
    resistance = GRAVITY * friction * jnp.sqrt(centre_x * centre_x + centre_y * centre_y) / (centre_depth * jnp.exp(jnp.log(centre_depth) * (4.0 / 3.0)))

    def along_x(f):
        return (f[:, 1:] - f[:, :-1]) / SPACING

    def along_y(f):
        return (f[1:, :] - f[:-1, :]) / SPACING
    change_depth = -(along_x(flux_x[0]) + along_y(flux_y[0]))
    change_x = -(along_x(flux_x[1]) + along_y(flux_y[2])) - GRAVITY * centre_depth * slope_x - resistance * centre_x
    change_y = -(along_x(flux_x[2]) + along_y(flux_y[1])) - GRAVITY * centre_depth * slope_y - resistance * centre_y
    return jnp.stack([change_depth, change_x, change_y]) * active

def friction_table(roughness):
    table = jnp.zeros(roughness.shape, jnp.float32)
    for level, value in enumerate(MANNING):
        table = table + jnp.where(roughness == level, value * value, 0.0)
    return table

def reflect_pad(field, rim_width, row_sign, col_sign):
    padded = jnp.pad(field, ((rim_width, rim_width), (0, 0)), mode='symmetric')
    places = jnp.arange(padded.shape[0])
    ghost = (places < rim_width) | (places >= padded.shape[0] - rim_width)
    padded = padded * jnp.where(ghost, row_sign, 1.0)[:, None]
    padded = jnp.pad(padded, ((0, 0), (rim_width, rim_width)), mode='symmetric')
    places = jnp.arange(padded.shape[1])
    ghost = (places < rim_width) | (places >= padded.shape[1] - rim_width)
    return padded * jnp.where(ghost, col_sign, 1.0)[None, :]

def grid_tendency(fields, bed_padded, flags, friction):
    padded = jnp.stack([reflect_pad(fields[i], 2, ROW_SIGNS[i], COL_SIGNS[i]) for i in range(3)])

    def row_band(band):
        first_row = band * TILE
        extended = lax.dynamic_slice_in_dim(padded, first_row, TILE + 4, axis=1)
        bed_band = lax.dynamic_slice_in_dim(bed_padded, first_row, TILE + 4, axis=0)
        active = jnp.broadcast_to(jnp.repeat(lax.dynamic_index_in_dim(flags, band, 0, keepdims=False), TILE), (TILE, NX))
        drag_band = jnp.broadcast_to(jnp.repeat(lax.dynamic_index_in_dim(friction, band, 0, keepdims=False), TILE), (TILE, NX))
        return tendency(extended, bed_band, drag_band, active, TILE, NX)
    bands = lax.map(row_band, jnp.arange(NTY, dtype=jnp.int32))
    return jnp.transpose(bands, (1, 0, 2, 3)).reshape(3, NY, NX)

def reference(water_state, bed_level, active_tiles, roughness):
    bed_padded = reflect_pad(bed_level, 2, 1.0, 1.0)
    friction = friction_table(roughness)
    fields = water_state
    for substep in range(SUBSTEPS):
        flags = active_tiles[substep].astype(jnp.float32)
        section_one = fields + TIME_STEP * grid_tendency(fields, bed_padded, flags, friction)
        fields = 0.5 * fields + 0.5 * (section_one + TIME_STEP * grid_tendency(section_one, bed_padded, flags, friction))
    return fields
```

```python
from functools import partial

import jax
import jax.numpy as jnp
from jax import lax
from jax.experimental import pallas as pl
from jax.experimental.pallas import tpu as pltpu
from jax.sharding import PartitionSpec as P

GRAVITY = 9.81
SPACING = 2.0
TIME_STEP = 0.1
MANNING = (0.03, 0.06, 0.1, 0.15)
MESH = pl.DeviceIdType.MESH
RIM = 4
PAD = 16
LANES = 128
ROWS = 8
GROUP = 4 * RIM


def minmod(a, b):
    return jnp.maximum(jnp.minimum(a, b), jnp.minimum(jnp.maximum(a, b), 0.0))


def physical(h, p, r):
    root = lax.rsqrt(h)
    u = p * (root * root)
    speed = jnp.abs(u) + (GRAVITY**0.5) * (h * root)
    return p * u + (0.5 * GRAVITY) * (h * h), r * u, speed


def twice_flux(left, right):
    l1, l2, lc = physical(*left)
    r1, r2, rc = physical(*right)
    c = jnp.maximum(lc, rc)
    return (
        (left[1] + right[1]) - c * (right[0] - left[0]),
        (l1 + r1) - c * (right[1] - left[1]),
        (l2 + r2) - c * (right[2] - left[2]),
    )


def after(x):
    return pltpu.roll(x, x.shape[1] - 1, 1)


def before(x):
    return pltpu.roll(x, 1, 1)


def lane_ids(shape):
    return lax.broadcasted_iota(jnp.int32, shape, 1)


def column_change(h, p, r):
    lefts, rights = [], []
    for v in (h, p, r):
        low = v - before(v)
        half = 0.5 * minmod(low, after(low))
        lefts.append(v + half)
        rights.append(after(v - half))
    return tuple(f - before(f) for f in twice_flux(lefts, rights))


def shifted(ref, f, start, width, moves):
    tall = ref[f, pl.ds(start - 8, ROWS + 16), :width]
    return [tall[8 + k : 8 + k + ROWS] for k in moves]


def row_fluxes(ref, start, width):
    lefts, rights = [], []
    for f in (0, 2, 1):
        a, b, c, d = shifted(ref, f, start, width, (-1, 0, 1, 2))
        ab, bc, cd = b - a, c - b, d - c
        lefts.append(b + 0.5 * minmod(ab, bc))
        rights.append(c - 0.5 * minmod(bc, cd))
    return twice_flux(lefts, rights)


def friction_of(level):
    value = jnp.float32(0.0)
    for number, n in enumerate(MANNING):
        value = jnp.where(level == number, jnp.float32(n * n), value)
    return value


def kernel(
    size,
    water,
    bed,
    active,
    roughness,
    out,
    fields,
    section,
    fluxes,
    slopes,
    scales,
    row_out,
    row_in,
    col_out,
    col_in,
    corner_in,
    load_sem,
    send_sem,
    recv_sem,
):
    rows, cols, n_rows, n_cols = size
    ring = cols + LANES
    a, b = lax.axis_index("gy"), lax.axis_index("gx")
    has_up, has_down, has_left, has_right = a > 0, a < n_rows - 1, b > 0, b < n_cols - 1
    first, last = PAD, PAD + rows

    load_water = pltpu.make_async_copy(
        water, fields.at[0:3, first:last, 0:cols], load_sem.at[0]
    )
    load_bed = pltpu.make_async_copy(bed, fields.at[3, first:last, 0:cols], load_sem.at[1])
    load_water.start()
    load_bed.start()

    barrier = pltpu.get_barrier_semaphore()
    around = (
        (has_up, -1, 0),
        (has_down, 1, 0),
        (has_left, 0, -1),
        (has_right, 0, 1),
        (has_up & has_left, -1, -1),
        (has_up & has_right, -1, 1),
        (has_down & has_left, 1, -1),
        (has_down & has_right, 1, 1),
    )
    for there, da, db in around:

        @pl.when(there)
        def _(da=da, db=db):
            pl.semaphore_signal(
                barrier, inc=1, device_id={"gy": a + da, "gx": b + db}, device_id_type=MESH
            )

    lanes = lane_ids((8, LANES))
    tiles = cols // rows
    n_tile_rows, n_tile_cols = active.shape[1], active.shape[2]

    def tile_factors(row, col):
        row = jnp.clip(row, 0, n_tile_rows - 1)
        col = jnp.clip(col, 0, n_tile_cols - 1)
        on = TIME_STEP * active[0, row, col].astype(jnp.float32)
        return -on / (2.0 * SPACING), -GRAVITY * on * friction_of(roughness[row, col])

    for place, row in enumerate((a - 1, a, a + 1)):
        for t in range(tiles):
            for kind, value in enumerate(tile_factors(row, b * tiles + t)):
                scales[place, kind, :, t * rows : (t + 1) * rows] = jnp.full((8, rows), value)
        right = tile_factors(row, (b + 1) * tiles)
        left = tile_factors(row, b * tiles - 1)
        for kind in range(2):
            scales[place, kind, :, cols:] = jnp.where(
                lanes < LANES // 2, right[kind], left[kind]
            )

    load_water.wait()
    load_bed.wait()

    for f in range(4):
        row_out[0, f * RIM : (f + 1) * RIM, :] = fields[f, first : first + RIM, 0:cols]
        row_out[1, f * RIM : (f + 1) * RIM, :] = fields[f, last - RIM : last, 0:cols]
    per_reg = LANES // GROUP
    blocks = rows // 8
    for side, (lane0, shift0) in enumerate(((0, 0), (cols - LANES, RIM))):
        for reg in range(blocks // per_reg):
            total = jnp.zeros((8, LANES), jnp.float32)
            for j in range(per_reg):
                row0 = first + 8 * (reg * per_reg + j)
                for f in range(4):
                    at = GROUP * j + RIM * f
                    v = fields[f, row0 : row0 + 8, lane0 : lane0 + LANES]
                    shift = (at + shift0) % LANES
                    v = pltpu.roll(v, shift, 1) if shift else v
                    total = jnp.where((lanes >= at) & (lanes < at + RIM), v, total)
            col_out[side, 8 * reg : 8 * reg + 8, :] = total
    place = lanes % RIM
    sign = jnp.where((lanes // RIM) % 4 == 1, -1.0, 1.0)
    for side in range(2):
        for reg in range(blocks // per_reg):
            x = col_out[side, 8 * reg : 8 * reg + 8, :]
            flipped = pltpu.roll(x, 3, 1)
            for c, shift in ((2, 1), (1, LANES - 1), (0, LANES - 3)):
                flipped = jnp.where(place == c, pltpu.roll(x, shift, 1), flipped)
            col_out[2 + side, 8 * reg : 8 * reg + 8, :] = flipped * sign

    pl.semaphore_wait(
        barrier,
        (1 + has_up.astype(jnp.int32) + has_down.astype(jnp.int32))
        * (1 + has_left.astype(jnp.int32) + has_right.astype(jnp.int32))
        - 1,
    )

    top = slice(0, 8)
    bottom = slice(rows // per_reg - 8, rows // per_reg)
    row_slots = lambda k: row_in.at[k]
    transfers = []

    def send(there, src, dst, slot, da, db):
        number = len(transfers)
        copy = pltpu.make_async_remote_copy(
            src_ref=src,
            dst_ref=dst,
            send_sem=send_sem.at[number],
            recv_sem=recv_sem.at[slot],
            device_id={"gy": a + da, "gx": b + db},
            device_id_type=MESH,
        )
        transfers.append((there, copy))

        @pl.when(there)
        def _():
            copy.start()

    send(has_down, row_out.at[1], row_slots(0), 0, 1, 0)
    send(has_up, row_out.at[0], row_slots(1), 1, -1, 0)
    send(has_right, col_out.at[1], col_in.at[0], 2, 0, 1)
    send(has_left, col_out.at[0], col_in.at[1], 3, 0, -1)
    send(has_down & has_right, col_out.at[1, bottom], corner_in.at[0], 4, 1, 1)
    send(has_down & has_left, col_out.at[0, bottom], corner_in.at[1], 5, 1, -1)
    send(has_up & has_right, col_out.at[1, top], corner_in.at[2], 6, -1, 1)
    send(has_up & has_left, col_out.at[0, top], corner_in.at[3], 7, -1, -1)
    no_left, no_right = b == 0, b == n_cols - 1
    send(has_down & no_left, col_out.at[2, bottom], corner_in.at[0], 4, 1, 0)
    send(has_down & no_right, col_out.at[3, bottom], corner_in.at[1], 5, 1, 0)
    send(has_up & no_left, col_out.at[2, top], corner_in.at[2], 6, -1, 0)
    send(has_up & no_right, col_out.at[3, top], corner_in.at[3], 7, -1, 0)

    def arrive(there, dst, slot):
        @pl.when(there)
        def _():
            pltpu.make_async_remote_copy(
                src_ref=dst,
                dst_ref=dst,
                send_sem=send_sem.at[0],
                recv_sem=recv_sem.at[slot],
                device_id={"gy": a, "gx": b},
                device_id_type=MESH,
            ).wait_recv()

    @pl.when(no_left)
    def _():
        col_in[0] = col_out[2]

    @pl.when(no_right)
    def _():
        col_in[1] = col_out[3]

    arrive(has_left, col_in.at[0], 2)
    arrive(has_right, col_in.at[1], 3)

    def unpack(left, right, j, f):
        at = GROUP * j + RIM * f
        right = pltpu.roll(right, (LANES - at) % LANES, 1) if at else right
        left = pltpu.roll(left, (2 * LANES - RIM - at) % LANES, 1)
        return jnp.where(lanes < LANES // 2, right, left)

    for reg in range(blocks // per_reg):
        left = col_in[0, 8 * reg : 8 * reg + 8, :]
        right = col_in[1, 8 * reg : 8 * reg + 8, :]
        for j in range(per_reg):
            row0 = first + 8 * (reg * per_reg + j)
            for f in range(4):
                fields[f, row0 : row0 + 8, cols:] = unpack(left, right, j, f)

    arrive(has_up, row_in.at[0], 0)
    arrive(has_up, corner_in.at[0], 4)
    arrive(has_up, corner_in.at[1], 5)
    arrive(has_down, row_in.at[1], 1)
    arrive(has_down, corner_in.at[2], 6)
    arrive(has_down, corner_in.at[3], 7)

    @pl.when(has_up)
    def _():
        for f in range(4):
            fields[f, first - 8 : first, cols:] = unpack(
                corner_in[0], corner_in[1], per_reg - 1, f
            )
            fields[f, first - RIM : first, 0:cols] = row_in[0, f * RIM : (f + 1) * RIM, :]

    @pl.when(has_down)
    def _():
        for f in range(4):
            fields[f, last : last + 8, cols:] = unpack(corner_in[2], corner_in[3], 0, f)
            fields[f, last : last + RIM, 0:cols] = row_in[1, f * RIM : (f + 1) * RIM, :]

    @pl.when(jnp.logical_not(has_up))
    def _():
        for f in range(4):
            for k in range(RIM):
                v = fields[f, first + k : first + k + 1, :]
                fields[f, first - 1 - k : first - k, :] = -v if f == 2 else v

    @pl.when(jnp.logical_not(has_down))
    def _():
        for f in range(4):
            for k in range(RIM):
                v = fields[f, last - 1 - k : last - k, :]
                fields[f, last + k : last + k + 1, :] = -v if f == 2 else v

    def flux_block(ref, start, width):
        for f, flux in enumerate(row_fluxes(ref, start, width)):
            fluxes[f, pl.ds(start, ROWS), :width] = flux

    def change(ref, start, width, place, gx, gy):
        h, p, r = (ref[f, pl.ds(start, ROWS), :] for f in range(3))
        x0, x1, x2 = (v[:, :width] for v in column_change(h, p, r))
        h, p, r = (v[:, :width] for v in (h, p, r))
        y0, y1, y2 = (
            below - above
            for below, above in (shifted(fluxes, f, start, width, (0, -1)) for f in range(3))
        )
        scale = scales[place, 0, :ROWS, :width]
        drag = scales[place, 1, :ROWS, :width]
        drag = drag * (jnp.sqrt(p * p + r * r) * jnp.exp(jnp.log(h) * (-7.0 / 3.0)))
        return (
            (h, p, r),
            (
                scale * (x0 + y0),
                scale * (x1 + y2 + h * gx) + drag * p,
                scale * (x2 + y1 + h * gy) + drag * r,
            ),
        )

    def first_block(start, place):
        level = fields[3, pl.ds(start, ROWS), :]
        gx = GRAVITY * (after(level) - before(level))
        south, north = shifted(fields, 3, start, ring, (1, -1))
        gy = GRAVITY * (south - north)
        slopes[0, pl.ds(start, ROWS), :] = gx
        slopes[1, pl.ds(start, ROWS), :] = gy
        state, rates = change(fields, start, ring, place, gx, gy)
        for f in range(3):
            section[f, pl.ds(start, ROWS), :] = state[f] + rates[f]

    def second_block(start):
        gx = slopes[0, pl.ds(start, ROWS), :cols]
        gy = slopes[1, pl.ds(start, ROWS), :cols]
        state, rates = change(section, start, cols, 1, gx, gy)
        for f in range(3):
            out[f, pl.ds(start - first, ROWS), :] = 0.5 * (
                fields[f, pl.ds(start, ROWS), :cols] + (state[f] + rates[f])
            )

    def each(begin, finish, work):
        def step(i, carry):
            work(pl.multiple_of(i * ROWS, 8))
            return carry

        lax.fori_loop(begin // ROWS, finish // ROWS, step, 0)

    each(first - 8, last + 8, lambda s: flux_block(fields, s, ring))
    first_block(first - 8, 0)
    each(first, last, lambda s: first_block(s, 1))
    first_block(last, 2)
    each(first - 8, last, lambda s: flux_block(section, s, cols))
    each(first, last, second_block)

    for there, copy in transfers:

        @pl.when(there)
        def _(copy=copy):
            copy.wait_send()


def body(n_rows, n_cols, water_state, bed_level, active_tiles, roughness):
    rows, cols = bed_level.shape
    ring, tall = cols + LANES, rows + 2 * PAD
    packed = rows * GROUP // LANES
    return pl.pallas_call(
        partial(kernel, (rows, cols, n_rows, n_cols)),
        out_shape=jax.ShapeDtypeStruct(water_state.shape, jnp.float32),
        in_specs=[
            pl.BlockSpec(memory_space=pl.ANY),
            pl.BlockSpec(memory_space=pl.ANY),
            pl.BlockSpec(memory_space=pltpu.SMEM),
            pl.BlockSpec(memory_space=pltpu.SMEM),
        ],
        out_specs=pl.BlockSpec(memory_space=pltpu.VMEM),
        scratch_shapes=[
            pltpu.VMEM((4, tall, ring), jnp.float32),
            pltpu.VMEM((3, tall, ring), jnp.float32),
            pltpu.VMEM((3, tall, ring), jnp.float32),
            pltpu.VMEM((2, tall, ring), jnp.float32),
            pltpu.VMEM((3, 2, 8, ring), jnp.float32),
            pltpu.VMEM((2, 4 * RIM, cols), jnp.float32),
            pltpu.VMEM((2, 4 * RIM, cols), jnp.float32),
            pltpu.VMEM((4, packed, LANES), jnp.float32),
            pltpu.VMEM((2, packed, LANES), jnp.float32),
            pltpu.VMEM((4, 8, LANES), jnp.float32),
            pltpu.SemaphoreType.DMA((2,)),
            pltpu.SemaphoreType.DMA((12,)),
            pltpu.SemaphoreType.DMA((8,)),
        ],
        compiler_params=pltpu.CompilerParams(
            collective_id=0, has_side_effects=True, vmem_limit_bytes=32 * 1024 * 1024
        ),
        cost_estimate=pl.CostEstimate(
            flops=400 * 3 * rows * cols, bytes_accessed=32 * rows * cols, transcendentals=0
        ),
    )(water_state, bed_level, active_tiles, roughness)


def solution(mesh):
    return jax.shard_map(
        partial(body, mesh.shape["gy"], mesh.shape["gx"]),
        mesh=mesh,
        in_specs=(P(None, "gy", "gx"), P("gy", "gx"), P(), P()),
        out_specs=P(None, "gy", "gx"),
        check_vma=False,
    )
```

```python
from functools import partial

import jax
import jax.numpy as jnp
from jax import lax
from jax.experimental import pallas as pl
from jax.experimental.pallas import tpu as pltpu
from jax.sharding import PartitionSpec as P

GRAVITY = 9.81
SPACING = 2.0
TIME_STEP = 0.1
MANNING = (0.03, 0.06, 0.1, 0.15)
MESH = pl.DeviceIdType.MESH
RIM = 4
PAD = 16
LANES = 128
STEP = 4
GROUP = 4 * RIM


def minmod(a, b):
    return jnp.maximum(jnp.minimum(a, b), jnp.minimum(jnp.maximum(a, b), 0.0))


def physical(h, p, r):
    root = lax.rsqrt(h)
    u = p * (root * root)
    speed = jnp.abs(u) + (GRAVITY**0.5) * (h * root)
    return p * u + (0.5 * GRAVITY) * (h * h), r * u, speed


def twice_flux(left, right):
    l1, l2, lc = physical(*left)
    r1, r2, rc = physical(*right)
    c = jnp.maximum(lc, rc)
    return (
        (left[1] + right[1]) - c * (right[0] - left[0]),
        (l1 + r1) - c * (right[1] - left[1]),
        (l2 + r2) - c * (right[2] - left[2]),
    )


def moved(x, by):
    return pltpu.roll(x, (-by) % x.shape[-1], x.ndim - 1)


def lane_ids(shape):
    return lax.broadcasted_iota(jnp.int32, shape, len(shape) - 1)


def faces(a, b, c, d):
    ab, bc, cd = b - a, c - b, d - c
    return b + 0.5 * minmod(ab, bc), c - 0.5 * minmod(bc, cd)


def column_change(h, p, r):
    sides = [faces(moved(v, -1), v, moved(v, 1), moved(v, 2)) for v in (h, p, r)]
    flux = twice_flux([s[0] for s in sides], [s[1] for s in sides])
    return tuple(f - moved(f, -1) for f in flux)


def row_fluxes(h, p, r):
    n = h.shape[0]
    sides = [faces(v[: n - 3], v[1 : n - 2], v[2 : n - 1], v[3:]) for v in (h, r, p)]
    return twice_flux([s[0] for s in sides], [s[1] for s in sides])


def friction_of(level):
    value = jnp.float32(0.0)
    for number, n in enumerate(MANNING):
        value = jnp.where(level == number, jnp.float32(n * n), value)
    return value


def kernel(
    size,
    water,
    bed,
    active_hbm,
    roughness_hbm,
    out,
    active,
    roughness,
    fields,
    tiled,
    section,
    slopes,
    result,
    scales,
    row_out,
    row_in,
    col_out,
    col_in,
    corner_in,
    load_sem,
    send_sem,
    recv_sem,
):
    rows, cols, n_rows, n_cols = size
    ring = cols + LANES
    a, b = lax.axis_index("gy"), lax.axis_index("gx")
    has_up, has_down, has_left, has_right = a > 0, a < n_rows - 1, b > 0, b < n_cols - 1
    first, last = PAD, PAD + rows

    panels = cols // LANES
    load_active = pltpu.make_async_copy(active_hbm, active, load_sem.at[0])
    load_roughness = pltpu.make_async_copy(roughness_hbm, roughness, load_sem.at[1])
    loads = []
    for c in range(panels):
        part = pl.ds(c * LANES, LANES)
        for src, dst in (
            (water.at[:, :, part], fields.at[0:3, c, first:last, :]),
            (bed.at[:, part], fields.at[3, c, first:last, :]),
        ):
            loads.append(pltpu.make_async_copy(src, dst, load_sem.at[2 + len(loads)]))
    for load in (load_active, load_roughness, *loads):
        load.start()

    barrier = pltpu.get_barrier_semaphore()
    around = (
        (has_up, -1, 0),
        (has_down, 1, 0),
        (has_left, 0, -1),
        (has_right, 0, 1),
        (has_up & has_left, -1, -1),
        (has_up & has_right, -1, 1),
        (has_down & has_left, 1, -1),
        (has_down & has_right, 1, 1),
    )
    for there, da, db in around:

        @pl.when(there)
        def _(da=da, db=db):
            pl.semaphore_signal(
                barrier, inc=1, device_id={"gy": a + da, "gx": b + db}, device_id_type=MESH
            )

    load_active.wait()
    load_roughness.wait()
    lanes = lane_ids((8, LANES))
    tiles = cols // rows
    n_tile_rows, n_tile_cols = active.shape[1], active.shape[2]

    def tile_factors(row, col):
        row = jnp.clip(row, 0, n_tile_rows - 1)
        col = jnp.clip(col, 0, n_tile_cols - 1)
        on = TIME_STEP * active[0, row, col].astype(jnp.float32)
        return -on / (2.0 * SPACING), -GRAVITY * on * friction_of(roughness[row, col])

    sublanes = lax.broadcasted_iota(jnp.int32, (8, LANES), 0)
    for place, row in ((1, a), (0, a - 1), (2, a + 1)):
        parts = [tile_factors(row, b * tiles + t) for t in range(tiles)]
        right = tile_factors(row, (b + 1) * tiles)
        left = tile_factors(row, b * tiles - 1)
        for kind in range(2):
            values = [
                jnp.full((8, LANES), parts[lane0 // rows][kind]) for lane0 in range(0, cols, LANES)
            ]
            values.append(jnp.where(lanes < LANES // 2, right[kind], left[kind]))
            for k, value in enumerate(values):
                at = slice(k * LANES, (k + 1) * LANES)
                if place != 1:
                    other = sublanes == (0 if place == 0 else 7)
                    value = jnp.where(other, value, scales[1, kind, :, at])
                scales[place, kind, :, at] = value

    for load in loads:
        load.wait()

    for f in range(4):
        for c in range(panels):
            at = slice(c * LANES, (c + 1) * LANES)
            row_out[0, f * RIM : (f + 1) * RIM, at] = fields[f, c, first : first + RIM]
            row_out[1, f * RIM : (f + 1) * RIM, at] = fields[f, c, last - RIM : last]
    per_reg = LANES // GROUP
    blocks = rows // 8
    for side, (panel, shift0) in enumerate(((0, 0), (panels - 1, RIM))):
        for reg in range(blocks // per_reg):
            total = jnp.zeros((8, LANES), jnp.float32)
            for j in range(per_reg):
                row0 = first + 8 * (reg * per_reg + j)
                for f in range(4):
                    at = GROUP * j + RIM * f
                    v = fields[f, panel, row0 : row0 + 8]
                    shift = (at + shift0) % LANES
                    v = pltpu.roll(v, shift, 1) if shift else v
                    total = jnp.where((lanes >= at) & (lanes < at + RIM), v, total)
            col_out[side, 8 * reg : 8 * reg + 8, :] = total
    place = lanes % RIM
    sign = jnp.where((lanes // RIM) % 4 == 1, -1.0, 1.0)
    for side in range(2):
        for reg in range(blocks // per_reg):
            x = col_out[side, 8 * reg : 8 * reg + 8, :]
            flipped = pltpu.roll(x, 3, 1)
            for c, shift in ((2, 1), (1, LANES - 1), (0, LANES - 3)):
                flipped = jnp.where(place == c, pltpu.roll(x, shift, 1), flipped)
            col_out[2 + side, 8 * reg : 8 * reg + 8, :] = flipped * sign

    pl.semaphore_wait(
        barrier,
        (1 + has_up.astype(jnp.int32) + has_down.astype(jnp.int32))
        * (1 + has_left.astype(jnp.int32) + has_right.astype(jnp.int32))
        - 1,
    )

    top = slice(0, 8)
    bottom = slice(rows // per_reg - 8, rows // per_reg)
    row_slots = lambda k: row_in.at[k]
    transfers = []

    def send(there, src, dst, slot, da, db):
        number = len(transfers)
        copy = pltpu.make_async_remote_copy(
            src_ref=src,
            dst_ref=dst,
            send_sem=send_sem.at[number],
            recv_sem=recv_sem.at[slot],
            device_id={"gy": a + da, "gx": b + db},
            device_id_type=MESH,
        )
        transfers.append((there, copy))

        @pl.when(there)
        def _():
            copy.start()

    send(has_down, row_out.at[1], row_slots(0), 0, 1, 0)
    send(has_up, row_out.at[0], row_slots(1), 1, -1, 0)
    send(has_right, col_out.at[1], col_in.at[0], 2, 0, 1)
    send(has_left, col_out.at[0], col_in.at[1], 3, 0, -1)
    send(has_down & has_right, col_out.at[1, bottom], corner_in.at[0], 4, 1, 1)
    send(has_down & has_left, col_out.at[0, bottom], corner_in.at[1], 5, 1, -1)
    send(has_up & has_right, col_out.at[1, top], corner_in.at[2], 6, -1, 1)
    send(has_up & has_left, col_out.at[0, top], corner_in.at[3], 7, -1, -1)
    no_left, no_right = b == 0, b == n_cols - 1
    send(has_down & no_left, col_out.at[2, bottom], corner_in.at[0], 4, 1, 0)
    send(has_down & no_right, col_out.at[3, bottom], corner_in.at[1], 5, 1, 0)
    send(has_up & no_left, col_out.at[2, top], corner_in.at[2], 6, -1, 0)
    send(has_up & no_right, col_out.at[3, top], corner_in.at[3], 7, -1, 0)

    def arrive(there, dst, slot):
        @pl.when(there)
        def _():
            pltpu.make_async_remote_copy(
                src_ref=dst,
                dst_ref=dst,
                send_sem=send_sem.at[0],
                recv_sem=recv_sem.at[slot],
                device_id={"gy": a, "gx": b},
                device_id_type=MESH,
            ).wait_recv()

    @pl.when(no_left)
    def _():
        col_in[0] = col_out[2]

    @pl.when(no_right)
    def _():
        col_in[1] = col_out[3]

    arrive(has_left, col_in.at[0], 2)
    arrive(has_right, col_in.at[1], 3)

    def unpack(left, right, j, f):
        at = GROUP * j + RIM * f
        right = pltpu.roll(right, (LANES - at) % LANES, 1) if at else right
        left = pltpu.roll(left, (2 * LANES - RIM - at) % LANES, 1)
        return jnp.where(lanes < LANES // 2, right, left)

    for reg in range(blocks // per_reg):
        left = col_in[0, 8 * reg : 8 * reg + 8, :]
        right = col_in[1, 8 * reg : 8 * reg + 8, :]
        for j in range(per_reg):
            row0 = first + 8 * (reg * per_reg + j)
            for f in range(4):
                fields[f, panels, row0 : row0 + 8] = unpack(left, right, j, f)

    arrive(has_up, row_in.at[0], 0)
    arrive(has_up, corner_in.at[0], 4)
    arrive(has_up, corner_in.at[1], 5)
    arrive(has_down, row_in.at[1], 1)
    arrive(has_down, corner_in.at[2], 6)
    arrive(has_down, corner_in.at[3], 7)

    @pl.when(has_up)
    def _():
        for f in range(4):
            fields[f, panels, first - 8 : first] = unpack(
                corner_in[0], corner_in[1], per_reg - 1, f
            )
            for c in range(panels):
                fields[f, c, first - RIM : first] = row_in[
                    0, f * RIM : (f + 1) * RIM, c * LANES : (c + 1) * LANES
                ]

    @pl.when(has_down)
    def _():
        for f in range(4):
            fields[f, panels, last : last + 8] = unpack(corner_in[2], corner_in[3], 0, f)
            for c in range(panels):
                fields[f, c, last : last + RIM] = row_in[
                    1, f * RIM : (f + 1) * RIM, c * LANES : (c + 1) * LANES
                ]

    @pl.when(jnp.logical_not(has_up))
    def _():
        for f in range(4):
            for k in range(RIM):
                v = fields[f, :, first + k : first + k + 1]
                fields[f, :, first - 1 - k : first - k] = -v if f == 2 else v

    @pl.when(jnp.logical_not(has_down))
    def _():
        for f in range(4):
            for k in range(RIM):
                v = fields[f, :, last - 1 - k : last - k]
                fields[f, :, last + k : last + k + 1] = -v if f == 2 else v

    stride = rows // 8

    for t in range(-RIM, stride + RIM):
        for f in range(4):
            for c in range(panels + 1):
                tiled[f, t + RIM, :, c * LANES : (c + 1) * LANES] = fields[
                    f, c, pl.ds(first + t, 8, stride), :
                ]

    def tiles_of(ref, f, t, count, origin, width):
        return ref[f, pl.ds(t + origin, count), :, :width]

    def fluxes_at(ref, t, count, origin, width):
        return row_fluxes(
            *(tiles_of(ref, f, t - 1, count + 3, origin, width) for f in range(3))
        )

    def section_rates(ref, t, count, origin, width, carry, scale, drag, gx, gy):
        h, p, r = (tiles_of(ref, f, t, count, origin, ring) for f in range(3))
        x0, x1, x2 = (v[..., :width] for v in column_change(h, p, r))
        h, p, r = (v[..., :width] for v in (h, p, r))
        below = fluxes_at(ref, t, count, origin, width)
        y0, y1, y2 = (
            now - jnp.concatenate([last_one, now[:-1]], axis=0)
            for now, last_one in zip(below, carry)
        )
        drag = drag * (jnp.sqrt(p * p + r * r) * jnp.exp(jnp.log(h) * (-7.0 / 3.0)))
        state = (
            h + scale * (x0 + y0),
            p + (scale * (x1 + y2 + h * gx) + drag * p),
            r + (scale * (x2 + y1 + h * gy) + drag * r),
        )
        return state, tuple(flux[-1:] for flux in below)

    def first_tiles(t, count, place, carry):
        level = tiles_of(tiled, 3, t, count, RIM, ring)
        gx = GRAVITY * (moved(level, 1) - moved(level, -1))
        gy = GRAVITY * (
            tiles_of(tiled, 3, t + 1, count, RIM, ring)
            - tiles_of(tiled, 3, t - 1, count, RIM, ring)
        )
        slopes[0, pl.ds(t + 2, count)] = gx
        slopes[1, pl.ds(t + 2, count)] = gy
        scale, drag = scales[place, 0][None], scales[place, 1][None]
        state, carry = section_rates(
            tiled, t, count, RIM, ring, carry, scale, drag, gx, gy
        )
        for f in range(3):
            section[f, pl.ds(t + 2, count)] = state[f]
        return carry

    def second_tiles(t, count, carry):
        gx = slopes[0, pl.ds(t + 2, count), :, :cols]
        gy = slopes[1, pl.ds(t + 2, count), :, :cols]
        scale, drag = scales[1, 0, :, :cols][None], scales[1, 1, :, :cols][None]
        state, carry = section_rates(
            section, t, count, 2, cols, carry, scale, drag, gx, gy
        )
        for f in range(3):
            final = 0.5 * (tiles_of(tiled, f, t, count, RIM, cols) + state[f])
            for k in range(count):
                for c in range(panels):
                    result[f, c, pl.ds(t + k, 8, stride), :] = final[
                        k, :, c * LANES : (c + 1) * LANES
                    ]
        return carry

    carry = fluxes_at(tiled, -3, 1, RIM, ring)
    carry = first_tiles(-2, 2, 0, carry)
    carry = lax.fori_loop(
        0, stride // STEP, lambda i, c: first_tiles(i * STEP, STEP, 1, c), carry
    )
    first_tiles(stride, 2, 2, carry)
    carry = fluxes_at(section, -1, 1, 2, cols)
    lax.fori_loop(0, stride // STEP, lambda i, c: second_tiles(i * STEP, STEP, c), carry)
    for c in range(panels):
        out[:, :, c * LANES : (c + 1) * LANES] = result[:, c]

    for there, copy in transfers:

        @pl.when(there)
        def _(copy=copy):
            copy.wait_send()


def body(n_rows, n_cols, water_state, bed_level, active_tiles, roughness):
    rows, cols = bed_level.shape
    ring, tall = cols + LANES, rows + 2 * PAD
    packed = rows * GROUP // LANES
    stride = rows // 8
    return pl.pallas_call(
        partial(kernel, (rows, cols, n_rows, n_cols)),
        out_shape=jax.ShapeDtypeStruct(water_state.shape, jnp.float32),
        in_specs=[
            pl.BlockSpec(memory_space=pltpu.HBM),
            pl.BlockSpec(memory_space=pltpu.HBM),
            pl.BlockSpec(memory_space=pltpu.HBM),
            pl.BlockSpec(memory_space=pltpu.HBM),
        ],
        out_specs=pl.BlockSpec(memory_space=pltpu.VMEM),
        scratch_shapes=[
            pltpu.SMEM(active_tiles.shape, jnp.int32),
            pltpu.SMEM(roughness.shape, jnp.int32),
            pltpu.VMEM((4, ring // LANES, tall, LANES), jnp.float32),
            pltpu.VMEM((4, stride + 2 * RIM, 8, ring), jnp.float32),
            pltpu.VMEM((3, stride + 4, 8, ring), jnp.float32),
            pltpu.VMEM((2, stride + 4, 8, ring), jnp.float32),
            pltpu.VMEM((3, cols // LANES, rows, LANES), jnp.float32),
            pltpu.VMEM((3, 2, 8, ring), jnp.float32),
            pltpu.VMEM((2, 4 * RIM, cols), jnp.float32),
            pltpu.VMEM((2, 4 * RIM, cols), jnp.float32),
            pltpu.VMEM((4, packed, LANES), jnp.float32),
            pltpu.VMEM((2, packed, LANES), jnp.float32),
            pltpu.VMEM((4, 8, LANES), jnp.float32),
            pltpu.SemaphoreType.DMA((2 + 2 * (cols // LANES),)),
            pltpu.SemaphoreType.DMA((12,)),
            pltpu.SemaphoreType.DMA((8,)),
        ],
        compiler_params=pltpu.CompilerParams(
            collective_id=0, has_side_effects=True, vmem_limit_bytes=24 * 1024 * 1024
        ),
        cost_estimate=pl.CostEstimate(
            flops=400 * 3 * rows * cols, bytes_accessed=32 * rows * cols, transcendentals=0
        ),
    )(water_state, bed_level, active_tiles, roughness)


def solution(mesh):
    return jax.shard_map(
        partial(body, mesh.shape["gy"], mesh.shape["gx"]),
        mesh=mesh,
        in_specs=(P(None, "gy", "gx"), P("gy", "gx"), P(), P()),
        out_specs=P(None, "gy", "gx"),
        check_vma=False,
    )
```

```python
from functools import partial

import jax
import jax.numpy as jnp
from jax import lax
from jax.experimental import pallas as pl
from jax.experimental.pallas import tpu as pltpu
from jax.sharding import PartitionSpec as P

GRAVITY = 9.81
SPACING = 2.0
TIME_STEP = 0.1
MANNING = (0.03, 0.06, 0.1, 0.15)
MESH = pl.DeviceIdType.MESH
RIM = 4
PAD = 16
LANES = 128
STEP = 4
GROUP = 4 * RIM


def minmod(a, b):
    return jnp.maximum(jnp.minimum(a, b), jnp.minimum(jnp.maximum(a, b), 0.0))


def physical(h, p, r):
    root = lax.rsqrt(h)
    u = p * (root * root)
    speed = jnp.abs(u) + (GRAVITY**0.5) * (h * root)
    return p * u + (0.5 * GRAVITY) * (h * h), r * u, speed


def twice_flux(left, right):
    l1, l2, lc = physical(*left)
    r1, r2, rc = physical(*right)
    c = jnp.maximum(lc, rc)
    return (
        (left[1] + right[1]) - c * (right[0] - left[0]),
        (l1 + r1) - c * (right[1] - left[1]),
        (l2 + r2) - c * (right[2] - left[2]),
    )


def moved(x, by):
    return pltpu.roll(x, (-by) % x.shape[-1], x.ndim - 1)


def lane_ids(shape):
    return lax.broadcasted_iota(jnp.int32, shape, len(shape) - 1)


def faces(a, b, c, d):
    ab, bc, cd = b - a, c - b, d - c
    return b + 0.5 * minmod(ab, bc), c - 0.5 * minmod(bc, cd)


def column_change(h, p, r):
    sides = [faces(moved(v, -1), v, moved(v, 1), moved(v, 2)) for v in (h, p, r)]
    flux = twice_flux([s[0] for s in sides], [s[1] for s in sides])
    return tuple(f - moved(f, -1) for f in flux)


def row_fluxes(h, p, r):
    n = h.shape[0]
    sides = [faces(v[: n - 3], v[1 : n - 2], v[2 : n - 1], v[3:]) for v in (h, r, p)]
    return twice_flux([s[0] for s in sides], [s[1] for s in sides])


def friction_of(level):
    value = jnp.float32(0.0)
    for number, n in enumerate(MANNING):
        value = jnp.where(level == number, jnp.float32(n * n), value)
    return value


def kernel(
    size,
    water,
    bed,
    active_hbm,
    roughness_hbm,
    out,
    active,
    roughness,
    fields,
    tiled,
    section,
    slopes,
    result,
    scales,
    row_out,
    row_in,
    col_out,
    col_in,
    corner_in,
    load_sem,
    send_sem,
    recv_sem,
):
    rows, cols, n_rows, n_cols = size
    ring = cols + LANES
    a, b = lax.axis_index("gy"), lax.axis_index("gx")
    has_up, has_down, has_left, has_right = a > 0, a < n_rows - 1, b > 0, b < n_cols - 1
    first, last = PAD, PAD + rows

    panels = cols // LANES
    load_active = pltpu.make_async_copy(active_hbm, active, load_sem.at[0])
    load_roughness = pltpu.make_async_copy(roughness_hbm, roughness, load_sem.at[1])
    loads = []
    for c in range(panels):
        part = pl.ds(c * LANES, LANES)
        for src, dst in (
            (water.at[:, :, part], fields.at[0:3, c, first:last, :]),
            (bed.at[:, part], fields.at[3, c, first:last, :]),
        ):
            loads.append(pltpu.make_async_copy(src, dst, load_sem.at[2 + len(loads)]))
    for load in (load_active, load_roughness, *loads):
        load.start()

    barrier = pltpu.get_barrier_semaphore()
    around = (
        (has_up, -1, 0),
        (has_down, 1, 0),
        (has_left, 0, -1),
        (has_right, 0, 1),
        (has_up & has_left, -1, -1),
        (has_up & has_right, -1, 1),
        (has_down & has_left, 1, -1),
        (has_down & has_right, 1, 1),
    )
    for there, da, db in around:

        @pl.when(there)
        def _(da=da, db=db):
            pl.semaphore_signal(
                barrier, inc=1, device_id={"gy": a + da, "gx": b + db}, device_id_type=MESH
            )

    load_active.wait()
    load_roughness.wait()
    lanes = lane_ids((8, LANES))
    tiles = cols // rows
    n_tile_rows, n_tile_cols = active.shape[1], active.shape[2]

    def tile_factors(row, col):
        row = jnp.clip(row, 0, n_tile_rows - 1)
        col = jnp.clip(col, 0, n_tile_cols - 1)
        on = TIME_STEP * active[0, row, col].astype(jnp.float32)
        return -on / (2.0 * SPACING), -GRAVITY * on * friction_of(roughness[row, col])

    sublanes = lax.broadcasted_iota(jnp.int32, (8, LANES), 0)
    for place, row in ((1, a), (0, a - 1), (2, a + 1)):
        parts = [tile_factors(row, b * tiles + t) for t in range(tiles)]
        right = tile_factors(row, (b + 1) * tiles)
        left = tile_factors(row, b * tiles - 1)
        for kind in range(2):
            values = [
                jnp.full((8, LANES), parts[lane0 // rows][kind]) for lane0 in range(0, cols, LANES)
            ]
            values.append(jnp.where(lanes < LANES // 2, right[kind], left[kind]))
            for k, value in enumerate(values):
                at = slice(k * LANES, (k + 1) * LANES)
                if place != 1:
                    other = sublanes == (0 if place == 0 else 7)
                    value = jnp.where(other, value, scales[1, kind, :, at])
                scales[place, kind, :, at] = value

    for load in loads:
        load.wait()

    for f in range(4):
        for c in range(panels):
            at = slice(c * LANES, (c + 1) * LANES)
            row_out[0, f * RIM : (f + 1) * RIM, at] = fields[f, c, first : first + RIM]
            row_out[1, f * RIM : (f + 1) * RIM, at] = fields[f, c, last - RIM : last]
    per_reg = LANES // GROUP
    blocks = rows // 8
    for side, (panel, shift0) in enumerate(((0, 0), (panels - 1, RIM))):
        for reg in range(blocks // per_reg):
            total = jnp.zeros((8, LANES), jnp.float32)
            for j in range(per_reg):
                row0 = first + 8 * (reg * per_reg + j)
                for f in range(4):
                    at = GROUP * j + RIM * f
                    v = fields[f, panel, row0 : row0 + 8]
                    shift = (at + shift0) % LANES
                    v = pltpu.roll(v, shift, 1) if shift else v
                    total = jnp.where((lanes >= at) & (lanes < at + RIM), v, total)
            col_out[side, 8 * reg : 8 * reg + 8, :] = total
    place = lanes % RIM
    sign = jnp.where((lanes // RIM) % 4 == 1, -1.0, 1.0)
    for side in range(2):
        for reg in range(blocks // per_reg):
            x = col_out[side, 8 * reg : 8 * reg + 8, :]
            flipped = pltpu.roll(x, 3, 1)
            for c, shift in ((2, 1), (1, LANES - 1), (0, LANES - 3)):
                flipped = jnp.where(place == c, pltpu.roll(x, shift, 1), flipped)
            col_out[2 + side, 8 * reg : 8 * reg + 8, :] = flipped * sign

    pl.semaphore_wait(
        barrier,
        (1 + has_up.astype(jnp.int32) + has_down.astype(jnp.int32))
        * (1 + has_left.astype(jnp.int32) + has_right.astype(jnp.int32))
        - 1,
    )

    top = slice(0, 8)
    bottom = slice(rows // per_reg - 8, rows // per_reg)
    row_slots = lambda k: row_in.at[k]
    transfers = []

    def send(there, src, dst, slot, da, db):
        number = len(transfers)
        copy = pltpu.make_async_remote_copy(
            src_ref=src,
            dst_ref=dst,
            send_sem=send_sem.at[number],
            recv_sem=recv_sem.at[slot],
            device_id={"gy": a + da, "gx": b + db},
            device_id_type=MESH,
        )
        transfers.append((there, copy))

        @pl.when(there)
        def _():
            copy.start()

    send(has_down, row_out.at[1], row_slots(0), 0, 1, 0)
    send(has_up, row_out.at[0], row_slots(1), 1, -1, 0)
    send(has_right, col_out.at[1], col_in.at[0], 2, 0, 1)
    send(has_left, col_out.at[0], col_in.at[1], 3, 0, -1)
    send(has_down & has_right, col_out.at[1, bottom], corner_in.at[0], 4, 1, 1)
    send(has_down & has_left, col_out.at[0, bottom], corner_in.at[1], 5, 1, -1)
    send(has_up & has_right, col_out.at[1, top], corner_in.at[2], 6, -1, 1)
    send(has_up & has_left, col_out.at[0, top], corner_in.at[3], 7, -1, -1)
    no_left, no_right = b == 0, b == n_cols - 1
    send(has_down & no_left, col_out.at[2, bottom], corner_in.at[0], 4, 1, 0)
    send(has_down & no_right, col_out.at[3, bottom], corner_in.at[1], 5, 1, 0)
    send(has_up & no_left, col_out.at[2, top], corner_in.at[2], 6, -1, 0)
    send(has_up & no_right, col_out.at[3, top], corner_in.at[3], 7, -1, 0)

    def arrive(there, dst, slot):
        @pl.when(there)
        def _():
            pltpu.make_async_remote_copy(
                src_ref=dst,
                dst_ref=dst,
                send_sem=send_sem.at[0],
                recv_sem=recv_sem.at[slot],
                device_id={"gy": a, "gx": b},
                device_id_type=MESH,
            ).wait_recv()

    @pl.when(no_left)
    def _():
        col_in[0] = col_out[2]

    @pl.when(no_right)
    def _():
        col_in[1] = col_out[3]

    arrive(has_left, col_in.at[0], 2)
    arrive(has_right, col_in.at[1], 3)

    def unpack(left, right, j, f):
        at = GROUP * j + RIM * f
        right = pltpu.roll(right, (LANES - at) % LANES, 1) if at else right
        left = pltpu.roll(left, (2 * LANES - RIM - at) % LANES, 1)
        return jnp.where(lanes < LANES // 2, right, left)

    for reg in range(blocks // per_reg):
        left = col_in[0, 8 * reg : 8 * reg + 8, :]
        right = col_in[1, 8 * reg : 8 * reg + 8, :]
        for j in range(per_reg):
            row0 = first + 8 * (reg * per_reg + j)
            for f in range(4):
                fields[f, panels, row0 : row0 + 8] = unpack(left, right, j, f)

    arrive(has_up, row_in.at[0], 0)
    arrive(has_up, corner_in.at[0], 4)
    arrive(has_up, corner_in.at[1], 5)
    arrive(has_down, row_in.at[1], 1)
    arrive(has_down, corner_in.at[2], 6)
    arrive(has_down, corner_in.at[3], 7)

    @pl.when(has_up)
    def _():
        for f in range(4):
            fields[f, panels, first - 8 : first] = unpack(
                corner_in[0], corner_in[1], per_reg - 1, f
            )
            for c in range(panels):
                fields[f, c, first - RIM : first] = row_in[
                    0, f * RIM : (f + 1) * RIM, c * LANES : (c + 1) * LANES
                ]

    @pl.when(has_down)
    def _():
        for f in range(4):
            fields[f, panels, last : last + 8] = unpack(corner_in[2], corner_in[3], 0, f)
            for c in range(panels):
                fields[f, c, last : last + RIM] = row_in[
                    1, f * RIM : (f + 1) * RIM, c * LANES : (c + 1) * LANES
                ]

    @pl.when(jnp.logical_not(has_up))
    def _():
        for f in range(4):
            for k in range(RIM):
                v = fields[f, :, first + k : first + k + 1]
                fields[f, :, first - 1 - k : first - k] = -v if f == 2 else v

    @pl.when(jnp.logical_not(has_down))
    def _():
        for f in range(4):
            for k in range(RIM):
                v = fields[f, :, last - 1 - k : last - k]
                fields[f, :, last + k : last + k + 1] = -v if f == 2 else v

    stride = rows // 8

    for t in range(-RIM, stride + RIM):
        for f in range(4):
            for c in range(panels + 1):
                tiled[f, t + RIM, :, c * LANES : (c + 1) * LANES] = fields[
                    f, c, pl.ds(first + t, 8, stride), :
                ]

    def tiles_of(ref, f, t, count, origin, width):
        return ref[f, pl.ds(t + origin, count), :, :width]

    def fluxes_at(ref, t, count, origin, width):
        return row_fluxes(
            *(tiles_of(ref, f, t - 1, count + 3, origin, width) for f in range(3))
        )

    def section_rates(ref, t, count, origin, width, carry, scale, drag, gx, gy):
        h, p, r = (tiles_of(ref, f, t, count, origin, ring) for f in range(3))
        x0, x1, x2 = (v[..., :width] for v in column_change(h, p, r))
        h, p, r = (v[..., :width] for v in (h, p, r))
        below = fluxes_at(ref, t, count, origin, width)
        y0, y1, y2 = (
            now - jnp.concatenate([last_one, now[:-1]], axis=0)
            for now, last_one in zip(below, carry)
        )
        drag = drag * (jnp.sqrt(p * p + r * r) * jnp.exp(jnp.log(h) * (-7.0 / 3.0)))
        state = (
            h + scale * (x0 + y0),
            p + (scale * (x1 + y2 + h * gx) + drag * p),
            r + (scale * (x2 + y1 + h * gy) + drag * r),
        )
        return state, tuple(flux[-1:] for flux in below)

    def first_tiles(t, count, place, carry):
        level = tiles_of(tiled, 3, t, count, RIM, ring)
        gx = GRAVITY * (moved(level, 1) - moved(level, -1))
        gy = GRAVITY * (
            tiles_of(tiled, 3, t + 1, count, RIM, ring)
            - tiles_of(tiled, 3, t - 1, count, RIM, ring)
        )
        slopes[0, pl.ds(t + 2, count)] = gx
        slopes[1, pl.ds(t + 2, count)] = gy
        scale, drag = scales[place, 0][None], scales[place, 1][None]
        state, carry = section_rates(
            tiled, t, count, RIM, ring, carry, scale, drag, gx, gy
        )
        for f in range(3):
            section[f, pl.ds(t + 2, count)] = state[f]
        return carry

    def second_tiles(t, count, carry):
        gx = slopes[0, pl.ds(t + 2, count), :, :cols]
        gy = slopes[1, pl.ds(t + 2, count), :, :cols]
        scale, drag = scales[1, 0, :, :cols][None], scales[1, 1, :, :cols][None]
        state, carry = section_rates(
            section, t, count, 2, cols, carry, scale, drag, gx, gy
        )
        for f in range(3):
            final = 0.5 * (tiles_of(tiled, f, t, count, RIM, cols) + state[f])
            for k in range(count):
                for c in range(panels):
                    result[f, c, pl.ds(t + k, 8, stride), :] = final[
                        k, :, c * LANES : (c + 1) * LANES
                    ]
        return carry

    carry = fluxes_at(tiled, -3, 1, RIM, ring)
    carry = first_tiles(-2, 2, 0, carry)
    carry = lax.fori_loop(
        0, stride // STEP, lambda i, c: first_tiles(i * STEP, STEP, 1, c), carry
    )
    first_tiles(stride, 2, 2, carry)
    carry = fluxes_at(section, -1, 1, 2, cols)
    lax.fori_loop(0, stride // STEP, lambda i, c: second_tiles(i * STEP, STEP, c), carry)
    stores = []
    for c in range(panels):
        stores.append(
            pltpu.make_async_copy(
                result.at[:, c], out.at[:, :, pl.ds(c * LANES, LANES)], load_sem.at[2 + c]
            )
        )
        stores[-1].start()
    for store in stores:
        store.wait()

    for there, copy in transfers:

        @pl.when(there)
        def _(copy=copy):
            copy.wait_send()


def body(n_rows, n_cols, water_state, bed_level, active_tiles, roughness):
    rows, cols = bed_level.shape
    ring, tall = cols + LANES, rows + 2 * PAD
    packed = rows * GROUP // LANES
    stride = rows // 8
    return pl.pallas_call(
        partial(kernel, (rows, cols, n_rows, n_cols)),
        out_shape=jax.ShapeDtypeStruct(water_state.shape, jnp.float32),
        in_specs=[
            pl.BlockSpec(memory_space=pl.ANY),
            pl.BlockSpec(memory_space=pl.ANY),
            pl.BlockSpec(memory_space=pl.ANY),
            pl.BlockSpec(memory_space=pl.ANY),
        ],
        out_specs=pl.BlockSpec(memory_space=pl.ANY),
        scratch_shapes=[
            pltpu.SMEM(active_tiles.shape, jnp.int32),
            pltpu.SMEM(roughness.shape, jnp.int32),
            pltpu.VMEM((4, ring // LANES, tall, LANES), jnp.float32),
            pltpu.VMEM((4, stride + 2 * RIM, 8, ring), jnp.float32),
            pltpu.VMEM((3, stride + 4, 8, ring), jnp.float32),
            pltpu.VMEM((2, stride + 4, 8, ring), jnp.float32),
            pltpu.VMEM((3, cols // LANES, rows, LANES), jnp.float32),
            pltpu.VMEM((3, 2, 8, ring), jnp.float32),
            pltpu.VMEM((2, 4 * RIM, cols), jnp.float32),
            pltpu.VMEM((2, 4 * RIM, cols), jnp.float32),
            pltpu.VMEM((4, packed, LANES), jnp.float32),
            pltpu.VMEM((2, packed, LANES), jnp.float32),
            pltpu.VMEM((4, 8, LANES), jnp.float32),
            pltpu.SemaphoreType.DMA((2 + 2 * (cols // LANES),)),
            pltpu.SemaphoreType.DMA((12,)),
            pltpu.SemaphoreType.DMA((8,)),
        ],
        compiler_params=pltpu.CompilerParams(
            collective_id=0, has_side_effects=True, vmem_limit_bytes=60 * 1024 * 1024
        ),
        cost_estimate=pl.CostEstimate(
            flops=400 * 3 * rows * cols, bytes_accessed=32 * rows * cols, transcendentals=0
        ),
    )(water_state, bed_level, active_tiles, roughness)


def solution(mesh):
    return jax.shard_map(
        partial(body, mesh.shape["gy"], mesh.shape["gx"]),
        mesh=mesh,
        in_specs=(P(None, "gy", "gx"), P("gy", "gx"), P(), P()),
        out_specs=P(None, "gy", "gx"),
        check_vma=False,
    )
```

```python
from functools import partial

import jax
import jax.numpy as jnp
from jax import lax
from jax.experimental import pallas as pl
from jax.experimental.pallas import tpu as pltpu
from jax.sharding import PartitionSpec as P

GRAVITY = 9.81
SPACING = 2.0
TIME_STEP = 0.1
MANNING = (0.03, 0.06, 0.1, 0.15)
MESH = pl.DeviceIdType.MESH
RIM = 4
PAD = 16
LANES = 128
STEP = 4
GROUP = 4 * RIM


def minmod(a, b):
    return jnp.maximum(jnp.minimum(a, b), jnp.minimum(jnp.maximum(a, b), 0.0))


def physical(h, p, r):
    root = lax.rsqrt(h)
    u = p * (root * root)
    speed = jnp.abs(u) + (GRAVITY**0.5) * (h * root)
    return p * u + (0.5 * GRAVITY) * (h * h), r * u, speed


def twice_flux(left, right):
    l1, l2, lc = physical(*left)
    r1, r2, rc = physical(*right)
    c = jnp.maximum(lc, rc)
    return (
        (left[1] + right[1]) - c * (right[0] - left[0]),
        (l1 + r1) - c * (right[1] - left[1]),
        (l2 + r2) - c * (right[2] - left[2]),
    )


def moved(x, by):
    return pltpu.roll(x, (-by) % x.shape[-1], x.ndim - 1)


def lane_ids(shape):
    return lax.broadcasted_iota(jnp.int32, shape, len(shape) - 1)


def faces(a, b, c, d):
    ab, bc, cd = b - a, c - b, d - c
    return b + 0.5 * minmod(ab, bc), c - 0.5 * minmod(bc, cd)


def column_change(h, p, r):
    sides = [faces(moved(v, -1), v, moved(v, 1), moved(v, 2)) for v in (h, p, r)]
    flux = twice_flux([s[0] for s in sides], [s[1] for s in sides])
    return tuple(f - moved(f, -1) for f in flux)


def row_fluxes(h, p, r):
    n = h.shape[0]
    sides = [faces(v[: n - 3], v[1 : n - 2], v[2 : n - 1], v[3:]) for v in (h, r, p)]
    return twice_flux([s[0] for s in sides], [s[1] for s in sides])


def friction_of(level):
    value = jnp.float32(0.0)
    for number, n in enumerate(MANNING):
        value = jnp.where(level == number, jnp.float32(n * n), value)
    return value


def kernel(
    size,
    water,
    bed,
    active_hbm,
    roughness_hbm,
    out,
    active,
    roughness,
    fields,
    tiled,
    section,
    fluxes,
    slopes,
    result,
    scales,
    row_out,
    row_in,
    col_out,
    col_in,
    corner_in,
    load_sem,
    send_sem,
    recv_sem,
):
    rows, cols, n_rows, n_cols = size
    ring = cols + LANES
    a, b = lax.axis_index("gy"), lax.axis_index("gx")
    has_up, has_down, has_left, has_right = a > 0, a < n_rows - 1, b > 0, b < n_cols - 1
    first, last = PAD, PAD + rows

    panels = cols // LANES
    load_active = pltpu.make_async_copy(active_hbm, active, load_sem.at[0])
    load_roughness = pltpu.make_async_copy(roughness_hbm, roughness, load_sem.at[1])
    loads = []
    for c in range(panels):
        part = pl.ds(c * LANES, LANES)
        for src, dst in (
            (water.at[:, :, part], fields.at[0:3, c, first:last, :]),
            (bed.at[:, part], fields.at[3, c, first:last, :]),
        ):
            loads.append(pltpu.make_async_copy(src, dst, load_sem.at[2 + len(loads)]))
    for load in (load_active, load_roughness, *loads):
        load.start()

    barrier = pltpu.get_barrier_semaphore()
    around = (
        (has_up, -1, 0),
        (has_down, 1, 0),
        (has_left, 0, -1),
        (has_right, 0, 1),
        (has_up & has_left, -1, -1),
        (has_up & has_right, -1, 1),
        (has_down & has_left, 1, -1),
        (has_down & has_right, 1, 1),
    )
    for there, da, db in around:

        @pl.when(there)
        def _(da=da, db=db):
            pl.semaphore_signal(
                barrier, inc=1, device_id={"gy": a + da, "gx": b + db}, device_id_type=MESH
            )

    load_active.wait()
    load_roughness.wait()
    lanes = lane_ids((8, LANES))
    tiles = cols // rows
    n_tile_rows, n_tile_cols = active.shape[1], active.shape[2]

    def tile_factors(row, col):
        row = jnp.clip(row, 0, n_tile_rows - 1)
        col = jnp.clip(col, 0, n_tile_cols - 1)
        on = TIME_STEP * active[0, row, col].astype(jnp.float32)
        return -on / (2.0 * SPACING), -GRAVITY * on * friction_of(roughness[row, col])

    sublanes = lax.broadcasted_iota(jnp.int32, (8, LANES), 0)
    for place, row in ((1, a), (0, a - 1), (2, a + 1)):
        parts = [tile_factors(row, b * tiles + t) for t in range(tiles)]
        right = tile_factors(row, (b + 1) * tiles)
        left = tile_factors(row, b * tiles - 1)
        for kind in range(2):
            values = [
                jnp.full((8, LANES), parts[lane0 // rows][kind]) for lane0 in range(0, cols, LANES)
            ]
            values.append(jnp.where(lanes < LANES // 2, right[kind], left[kind]))
            for k, value in enumerate(values):
                at = slice(k * LANES, (k + 1) * LANES)
                if place != 1:
                    other = sublanes == (0 if place == 0 else 7)
                    value = jnp.where(other, value, scales[1, kind, :, at])
                scales[place, kind, :, at] = value

    for load in loads:
        load.wait()

    for f in range(4):
        for c in range(panels):
            at = slice(c * LANES, (c + 1) * LANES)
            row_out[0, f * RIM : (f + 1) * RIM, at] = fields[f, c, first : first + RIM]
            row_out[1, f * RIM : (f + 1) * RIM, at] = fields[f, c, last - RIM : last]
    per_reg = LANES // GROUP
    blocks = rows // 8
    for side, (panel, shift0) in enumerate(((0, 0), (panels - 1, RIM))):
        for reg in range(blocks // per_reg):
            total = jnp.zeros((8, LANES), jnp.float32)
            for j in range(per_reg):
                row0 = first + 8 * (reg * per_reg + j)
                for f in range(4):
                    at = GROUP * j + RIM * f
                    v = fields[f, panel, row0 : row0 + 8]
                    shift = (at + shift0) % LANES
                    v = pltpu.roll(v, shift, 1) if shift else v
                    total = jnp.where((lanes >= at) & (lanes < at + RIM), v, total)
            col_out[side, 8 * reg : 8 * reg + 8, :] = total
    place = lanes % RIM
    sign = jnp.where((lanes // RIM) % 4 == 1, -1.0, 1.0)
    for side in range(2):
        for reg in range(blocks // per_reg):
            x = col_out[side, 8 * reg : 8 * reg + 8, :]
            flipped = pltpu.roll(x, 3, 1)
            for c, shift in ((2, 1), (1, LANES - 1), (0, LANES - 3)):
                flipped = jnp.where(place == c, pltpu.roll(x, shift, 1), flipped)
            col_out[2 + side, 8 * reg : 8 * reg + 8, :] = flipped * sign

    pl.semaphore_wait(
        barrier,
        (1 + has_up.astype(jnp.int32) + has_down.astype(jnp.int32))
        * (1 + has_left.astype(jnp.int32) + has_right.astype(jnp.int32))
        - 1,
    )

    top = slice(0, 8)
    bottom = slice(rows // per_reg - 8, rows // per_reg)
    row_slots = lambda k: row_in.at[k]
    transfers = []

    def send(there, src, dst, slot, da, db):
        number = len(transfers)
        copy = pltpu.make_async_remote_copy(
            src_ref=src,
            dst_ref=dst,
            send_sem=send_sem.at[number],
            recv_sem=recv_sem.at[slot],
            device_id={"gy": a + da, "gx": b + db},
            device_id_type=MESH,
        )
        transfers.append((there, copy))

        @pl.when(there)
        def _():
            copy.start()

    send(has_down, row_out.at[1], row_slots(0), 0, 1, 0)
    send(has_up, row_out.at[0], row_slots(1), 1, -1, 0)
    send(has_right, col_out.at[1], col_in.at[0], 2, 0, 1)
    send(has_left, col_out.at[0], col_in.at[1], 3, 0, -1)
    send(has_down & has_right, col_out.at[1, bottom], corner_in.at[0], 4, 1, 1)
    send(has_down & has_left, col_out.at[0, bottom], corner_in.at[1], 5, 1, -1)
    send(has_up & has_right, col_out.at[1, top], corner_in.at[2], 6, -1, 1)
    send(has_up & has_left, col_out.at[0, top], corner_in.at[3], 7, -1, -1)
    no_left, no_right = b == 0, b == n_cols - 1
    send(has_down & no_left, col_out.at[2, bottom], corner_in.at[0], 4, 1, 0)
    send(has_down & no_right, col_out.at[3, bottom], corner_in.at[1], 5, 1, 0)
    send(has_up & no_left, col_out.at[2, top], corner_in.at[2], 6, -1, 0)
    send(has_up & no_right, col_out.at[3, top], corner_in.at[3], 7, -1, 0)

    stride = rows // 8

    def retile(t, panel_range):
        for f in range(4):
            for c in panel_range:
                tiled[f, t + RIM, :, c * LANES : (c + 1) * LANES] = fields[
                    f, c, pl.ds(first + t, 8, stride), :
                ]

    def keep_fluxes(t, count, lane0, lane1):
        values = row_fluxes(
            *(tiled[f, pl.ds(t - 1 + RIM, count + 3), :, lane0:lane1] for f in range(3))
        )
        for f in range(3):
            fluxes[f, pl.ds(t + 3, count), :, lane0:lane1] = values[f]

    for t in range(stride):
        retile(t, range(panels))
    for t in range(1, stride - 2, STEP):
        keep_fluxes(t, min(STEP, stride - 2 - t), 0, cols)

    def arrive(there, dst, slot):
        @pl.when(there)
        def _():
            pltpu.make_async_remote_copy(
                src_ref=dst,
                dst_ref=dst,
                send_sem=send_sem.at[0],
                recv_sem=recv_sem.at[slot],
                device_id={"gy": a, "gx": b},
                device_id_type=MESH,
            ).wait_recv()

    @pl.when(no_left)
    def _():
        col_in[0] = col_out[2]

    @pl.when(no_right)
    def _():
        col_in[1] = col_out[3]

    arrive(has_left, col_in.at[0], 2)
    arrive(has_right, col_in.at[1], 3)

    def unpack(left, right, j, f):
        at = GROUP * j + RIM * f
        right = pltpu.roll(right, (LANES - at) % LANES, 1) if at else right
        left = pltpu.roll(left, (2 * LANES - RIM - at) % LANES, 1)
        return jnp.where(lanes < LANES // 2, right, left)

    for reg in range(blocks // per_reg):
        left = col_in[0, 8 * reg : 8 * reg + 8, :]
        right = col_in[1, 8 * reg : 8 * reg + 8, :]
        for j in range(per_reg):
            row0 = first + 8 * (reg * per_reg + j)
            for f in range(4):
                fields[f, panels, row0 : row0 + 8] = unpack(left, right, j, f)

    arrive(has_up, row_in.at[0], 0)
    arrive(has_up, corner_in.at[0], 4)
    arrive(has_up, corner_in.at[1], 5)
    arrive(has_down, row_in.at[1], 1)
    arrive(has_down, corner_in.at[2], 6)
    arrive(has_down, corner_in.at[3], 7)

    @pl.when(has_up)
    def _():
        for f in range(4):
            fields[f, panels, first - 8 : first] = unpack(
                corner_in[0], corner_in[1], per_reg - 1, f
            )
            for c in range(panels):
                fields[f, c, first - RIM : first] = row_in[
                    0, f * RIM : (f + 1) * RIM, c * LANES : (c + 1) * LANES
                ]

    @pl.when(has_down)
    def _():
        for f in range(4):
            fields[f, panels, last : last + 8] = unpack(corner_in[2], corner_in[3], 0, f)
            for c in range(panels):
                fields[f, c, last : last + RIM] = row_in[
                    1, f * RIM : (f + 1) * RIM, c * LANES : (c + 1) * LANES
                ]

    @pl.when(jnp.logical_not(has_up))
    def _():
        for f in range(4):
            for k in range(RIM):
                v = fields[f, :, first + k : first + k + 1]
                fields[f, :, first - 1 - k : first - k] = -v if f == 2 else v

    @pl.when(jnp.logical_not(has_down))
    def _():
        for f in range(4):
            for k in range(RIM):
                v = fields[f, :, last - 1 - k : last - k]
                fields[f, :, last + k : last + k + 1] = -v if f == 2 else v


    for t in range(-RIM, stride + RIM):
        retile(t, range(panels, panels + 1) if 0 <= t < stride else range(panels + 1))

    def tiles_of(ref, f, t, count, origin, width):
        return ref[f, pl.ds(t + origin, count), :, :width]

    def fluxes_at(ref, t, count, origin, width):
        return row_fluxes(
            *(tiles_of(ref, f, t - 1, count + 3, origin, width) for f in range(3))
        )

    def section_rates(ref, t, count, origin, width, carry, scale, drag, gx, gy):
        h, p, r = (tiles_of(ref, f, t, count, origin, ring) for f in range(3))
        x0, x1, x2 = (v[..., :width] for v in column_change(h, p, r))
        h, p, r = (v[..., :width] for v in (h, p, r))
        if ref is tiled:
            below = tuple(fluxes[f, pl.ds(t + 3, count)] for f in range(3))
        else:
            below = fluxes_at(ref, t, count, origin, width)
        y0, y1, y2 = (
            now - jnp.concatenate([last_one, now[:-1]], axis=0)
            for now, last_one in zip(below, carry)
        )
        drag = drag * (jnp.sqrt(p * p + r * r) * jnp.exp(jnp.log(h) * (-7.0 / 3.0)))
        state = (
            h + scale * (x0 + y0),
            p + (scale * (x1 + y2 + h * gx) + drag * p),
            r + (scale * (x2 + y1 + h * gy) + drag * r),
        )
        return state, tuple(flux[-1:] for flux in below)

    def first_tiles(t, count, place, carry):
        level = tiles_of(tiled, 3, t, count, RIM, ring)
        gx = GRAVITY * (moved(level, 1) - moved(level, -1))
        gy = GRAVITY * (
            tiles_of(tiled, 3, t + 1, count, RIM, ring)
            - tiles_of(tiled, 3, t - 1, count, RIM, ring)
        )
        slopes[0, pl.ds(t + 2, count)] = gx
        slopes[1, pl.ds(t + 2, count)] = gy
        scale, drag = scales[place, 0][None], scales[place, 1][None]
        state, carry = section_rates(
            tiled, t, count, RIM, ring, carry, scale, drag, gx, gy
        )
        for f in range(3):
            section[f, pl.ds(t + 2, count)] = state[f]
        return carry

    def second_tiles(t, count, carry):
        gx = slopes[0, pl.ds(t + 2, count), :, :cols]
        gy = slopes[1, pl.ds(t + 2, count), :, :cols]
        scale, drag = scales[1, 0, :, :cols][None], scales[1, 1, :, :cols][None]
        state, carry = section_rates(
            section, t, count, 2, cols, carry, scale, drag, gx, gy
        )
        for f in range(3):
            final = 0.5 * (tiles_of(tiled, f, t, count, RIM, cols) + state[f])
            for k in range(count):
                for c in range(panels):
                    result[f, c, pl.ds(t + k, 8, stride), :] = final[
                        k, :, c * LANES : (c + 1) * LANES
                    ]
        return carry

    keep_fluxes(-3, 4, 0, ring)
    keep_fluxes(stride - 2, 4, 0, ring)
    keep_fluxes(1, stride - 3, cols, ring)
    carry = tuple(fluxes[f, pl.ds(0, 1)] for f in range(3))
    carry = first_tiles(-2, 2, 0, carry)
    carry = lax.fori_loop(
        0, stride // STEP, lambda i, c: first_tiles(i * STEP, STEP, 1, c), carry
    )
    first_tiles(stride, 2, 2, carry)
    carry = fluxes_at(section, -1, 1, 2, cols)
    lax.fori_loop(0, stride // STEP, lambda i, c: second_tiles(i * STEP, STEP, c), carry)
    stores = []
    for c in range(panels):
        stores.append(
            pltpu.make_async_copy(
                result.at[:, c], out.at[:, :, pl.ds(c * LANES, LANES)], load_sem.at[2 + c]
            )
        )
        stores[-1].start()
    for store in stores:
        store.wait()

    for there, copy in transfers:

        @pl.when(there)
        def _(copy=copy):
            copy.wait_send()


def body(n_rows, n_cols, water_state, bed_level, active_tiles, roughness):
    rows, cols = bed_level.shape
    ring, tall = cols + LANES, rows + 2 * PAD
    packed = rows * GROUP // LANES
    stride = rows // 8
    return pl.pallas_call(
        partial(kernel, (rows, cols, n_rows, n_cols)),
        out_shape=jax.ShapeDtypeStruct(water_state.shape, jnp.float32),
        in_specs=[
            pl.BlockSpec(memory_space=pl.ANY),
            pl.BlockSpec(memory_space=pl.ANY),
            pl.BlockSpec(memory_space=pl.ANY),
            pl.BlockSpec(memory_space=pl.ANY),
        ],
        out_specs=pl.BlockSpec(memory_space=pl.ANY),
        scratch_shapes=[
            pltpu.SMEM(active_tiles.shape, jnp.int32),
            pltpu.SMEM(roughness.shape, jnp.int32),
            pltpu.VMEM((4, ring // LANES, tall, LANES), jnp.float32),
            pltpu.VMEM((4, stride + 2 * RIM, 8, ring), jnp.float32),
            pltpu.VMEM((3, stride + 4, 8, ring), jnp.float32),
            pltpu.VMEM((3, stride + 5, 8, ring), jnp.float32),
            pltpu.VMEM((2, stride + 4, 8, ring), jnp.float32),
            pltpu.VMEM((3, cols // LANES, rows, LANES), jnp.float32),
            pltpu.VMEM((3, 2, 8, ring), jnp.float32),
            pltpu.VMEM((2, 4 * RIM, cols), jnp.float32),
            pltpu.VMEM((2, 4 * RIM, cols), jnp.float32),
            pltpu.VMEM((4, packed, LANES), jnp.float32),
            pltpu.VMEM((2, packed, LANES), jnp.float32),
            pltpu.VMEM((4, 8, LANES), jnp.float32),
            pltpu.SemaphoreType.DMA((2 + 2 * (cols // LANES),)),
            pltpu.SemaphoreType.DMA((12,)),
            pltpu.SemaphoreType.DMA((8,)),
        ],
        compiler_params=pltpu.CompilerParams(
            collective_id=0, has_side_effects=True, vmem_limit_bytes=60 * 1024 * 1024
        ),
        cost_estimate=pl.CostEstimate(
            flops=400 * 3 * rows * cols, bytes_accessed=32 * rows * cols, transcendentals=0
        ),
    )(water_state, bed_level, active_tiles, roughness)


def solution(mesh):
    return jax.shard_map(
        partial(body, mesh.shape["gy"], mesh.shape["gx"]),
        mesh=mesh,
        in_specs=(P(None, "gy", "gx"), P("gy", "gx"), P(), P()),
        out_specs=P(None, "gy", "gx"),
        check_vma=False,
    )
```
